512 devices in a mesh: dp: 64 (over y, z_lo, core), ctx: 8 (over x, z_hi).
Axes of the slice: x: 4, y: 8, z: 8 (z_hi: 2, z_lo: 4; z = z_hi * 4 + z_lo), core: 2. Of those that a mesh axis runs over, the one named last changes fastest.
Arguments:
- query_states: bfloat16 [64, 1024, 5120], P('dp', 'ctx'), may hold values from -64 to 64
- key_states: bfloat16 [64, 1024, 1024], P('dp', 'ctx'), may hold values from -16 to 16
- out_grad: bfloat16 [64, 1024, 5120], P('dp', 'ctx'), may hold values from -6 to 6
- layer_input: bfloat16 [64, 1024, 5120], P('dp', 'ctx'), may hold values from -6 to 6
- block_mask: int32 [64, 8, 8], P('dp'), may hold values from 0 to 1, as said below
Outputs:
- value_grad: bfloat16 [64, 1024, 1024], P('dp', 'ctx')
- weight_grad: float32 [5120, 1024], P('dp', 'ctx')
The draws below stay inside these ranges and needn't reach their ends.
Inputs may be any that keep to these rules, and one draw needn't show every extreme that they name: block_mask[b] is the ancestor relation of a forest over the 8 blocks of sequence b: entry (r, c) is 1 exactly when block c is block r or an ancestor of it, and every block's parent comes before it.
All inputs are finite; a program needn't handle non-finite values.
Results may differ from the reference program's by a relative error of at most 0.0048.
Values may be sent and summed in bfloat16 or wider, within the bound.
A program may use at most 64 MiB of HBM per device.

```python
import math
import jax
import jax.numpy as jnp
from jax import lax

MODEL_WIDTH = 5120
HQ = 40
KEY_VALUE_HEADS = 8
HEAD_SIZE = 128
BLK = 128
GROUP = 5
SEQUENCE_LENGTH = 1024
NB = 8
PACKED_BATCH = 64


def key_noise(key):
    return jax.random.normal(jax.random.fold_in(key, 11), (PACKED_BATCH, SEQUENCE_LENGTH, KEY_VALUE_HEADS, HEAD_SIZE), jnp.float32)


def draw_key_states(key, part):
    noise = key_noise(key)
    hidden_states = noise
    hidden_states = jnp.clip(hidden_states, -16.0, 16.0)
    return hidden_states.reshape(PACKED_BATCH, SEQUENCE_LENGTH, KEY_VALUE_HEADS * HEAD_SIZE).astype(jnp.bfloat16)


def draw_query_states(key, part):
    key = jax.random.fold_in(key, 2)
    hidden_states = jax.random.normal(key, (PACKED_BATCH, SEQUENCE_LENGTH, HQ, HEAD_SIZE), jnp.float32)
    hidden_states = jnp.clip(hidden_states, -64.0, 64.0)
    return hidden_states.reshape(PACKED_BATCH, SEQUENCE_LENGTH, HQ * HEAD_SIZE).astype(jnp.bfloat16)


def draw_block_mask(key, part):
    key = jax.random.fold_in(key, 3)
    node_kind = jax.random.randint(key, (PACKED_BATCH, NB), 0, 4)
    spread = jax.random.randint(jax.random.fold_in(key, 1), (PACKED_BATCH, NB), 0, 1 << 20)
    row_ids = jnp.arange(NB)
    earlier = spread % jnp.maximum(row_ids, 1)[None, :]
    parent = jnp.where(node_kind == 0, -1, jnp.where(node_kind == 1, earlier, row_ids[None, :] - 1))
    parent = jnp.where(row_ids[None, :] == 0, -1, parent)
    batch_ids = jnp.arange(PACKED_BATCH)

    def add_row(step_row, ancestry):
        parent_now = parent[:, step_row]
        parent_safe = jnp.maximum(parent_now, 0)
        inherited = ancestry[batch_ids, parent_safe]
        inherited = jnp.where((parent_now >= 0)[:, None], inherited, 0)
        own_bit = (row_ids == step_row).astype(jnp.int32)[None, :]
        return ancestry.at[:, step_row, :].set(inherited + own_bit)
    start_offset = jnp.zeros((PACKED_BATCH, NB, NB), jnp.int32)
    return lax.fori_loop(0, NB, add_row, start_offset)


def block_levels(own_key, extent, pieces, low, largest):
    loudness, own = 1.0, jax.random.fold_in(own_key, 6)
    for axis_at, shards_of in pieces:
        heights = jnp.exp(jax.random.uniform(jax.random.fold_in(own, axis_at), (shards_of,), jnp.float32, low / len(pieces), largest / len(pieces)))
        loudness = loudness * jnp.repeat(heights, extent[axis_at] // shards_of).reshape([-1 if axis == axis_at else 1 for axis in range(len(extent))])
    return loudness


def normal_values(stream_key, dims, deviation, limit, pieces=(), kind=jnp.bfloat16):
    entries = deviation * jax.random.normal(stream_key, dims, jnp.float32)
    if pieces:
        entries = entries * block_levels(stream_key, dims, pieces, -0.22, 0.18)
    return jnp.clip(entries, -limit, limit).astype(kind)


def setup_inputs(seed: int = 0) -> dict:
    streams_of = jax.random.split(jax.random.key(seed), 6)
    query_states = draw_query_states(jax.random.fold_in(streams_of[5], 71), 0)
    key_states = draw_key_states(jax.random.fold_in(streams_of[5], 71), 0)
    out_grad = normal_values(streams_of[2], (PACKED_BATCH, SEQUENCE_LENGTH, HQ * HEAD_SIZE), 1.0, 6.0, ((0, 64), (1, 8)))
    layer_input = normal_values(streams_of[3], (PACKED_BATCH, SEQUENCE_LENGTH, MODEL_WIDTH), 1.0, 6.0, ((0, 64), (1, 8)))
    block_mask = draw_block_mask(jax.random.fold_in(streams_of[5], 71), 0)
    return dict(query_states=query_states, key_states=key_states, out_grad=out_grad, layer_input=layer_input, block_mask=block_mask)


def one_sequence(inputs):
    queries, keys_all, grads, mask_table = inputs
    positions = jnp.arange(SEQUENCE_LENGTH)
    block_ids = positions // BLK
    visible = (mask_table[block_ids][:, block_ids] == 1) & (positions[None, :] <= positions[:, None])
    inv_root = 1.0 / math.sqrt(HEAD_SIZE)

    def single_head_group(kv_index):
        key_cols = lax.dynamic_slice_in_dim(keys_all, kv_index * HEAD_SIZE, HEAD_SIZE, 1).astype(jnp.float32)
        query_cols = lax.dynamic_slice_in_dim(queries, kv_index * GROUP * HEAD_SIZE, GROUP * HEAD_SIZE, 1)
        query_cols = query_cols.reshape(SEQUENCE_LENGTH, GROUP, HEAD_SIZE).astype(jnp.float32)
        grad_cols = lax.dynamic_slice_in_dim(grads, kv_index * GROUP * HEAD_SIZE, GROUP * HEAD_SIZE, 1)
        grad_cols = grad_cols.reshape(SEQUENCE_LENGTH, GROUP, HEAD_SIZE).astype(jnp.float32)
        scores = jnp.einsum('qgd,kd->gqk', query_cols, key_cols) * inv_root
        masked = jnp.where(visible[None], scores, -jnp.inf)
        row_max = lax.optimization_barrier(jnp.max(masked, axis=2, keepdims=True))
        log_total = row_max + jnp.log(lax.optimization_barrier(jnp.sum(jnp.exp(masked - row_max), axis=2, keepdims=True)))
        weights = jnp.exp(masked - log_total).astype(jnp.bfloat16)
        return jnp.einsum('gqk,qgd->kd', weights.astype(jnp.float32), grad_cols)
    each_head_rows = lax.map(single_head_group, jnp.arange(KEY_VALUE_HEADS, dtype=jnp.int32))
    return jnp.transpose(each_head_rows, (1, 0, 2)).reshape(SEQUENCE_LENGTH, KEY_VALUE_HEADS * HEAD_SIZE).astype(jnp.bfloat16)

def reference(query_states, key_states, out_grad, layer_input, block_mask):
    value_grad = lax.map(one_sequence, (query_states, key_states, out_grad, block_mask))

    def add_sequence(running, pair):
        inputs_seq, grads_seq = pair
        return (running + jnp.dot(inputs_seq.T, grads_seq, preferred_element_type=jnp.float32), None)
    start_offset = jnp.zeros((MODEL_WIDTH, KEY_VALUE_HEADS * HEAD_SIZE), jnp.float32)
    summed, unused = lax.scan(add_sequence, start_offset, (layer_input, value_grad))
    return (value_grad, summed / PACKED_BATCH)
```

```python
import functools
import math

import jax
import jax.numpy as jnp
from jax import lax
from jax.experimental import pallas as pl
from jax.experimental.pallas import tpu as pltpu
from jax.sharding import PartitionSpec as P

HEAD = 128
GROUP = 5
BF16 = jnp.bfloat16
F32 = jnp.float32
MESH = pl.DeviceIdType.MESH
HIDDEN = -1e30


def kernel(
    q_ref, k_ref, g_ref, x_ref, mask_ref, vgrad_ref, wgrad_ref,
    qb, gb, kb, xb, xt, bias, vacc, vsend, vrecv, v2, ca, cb, ra, rb, sa, sb, fin,
    own_sem, k_ss, k_rs, q_ss, q_rs, g_ss, g_rs, x_ss, x_rs, z_ss, z_rs, a_ss, a_rs,
    f_ss, f_rs, ra_ss, ra_rs, rb_ss, rb_rs, fin_ss, fin_rs,
):
    d = lax.axis_index("dp")
    t = lax.axis_index("ctx")
    core = lax.rem(d, 2)
    zl = lax.rem(lax.div(d, 2), 4)
    y = lax.div(d, 8)
    x = lax.div(t, 2)
    zh = lax.rem(t, 2)
    z = zh * 4 + zl
    d_core = d + 1 - 2 * core
    y_odd = lax.rem(y, 2)
    z_odd = lax.rem(z, 2)

    def place(px, py, pz, pc):
        return ((py * 4 + lax.rem(pz, 4)) * 2 + pc, px * 2 + lax.div(pz, 4))

    def mine(px, py, pz, pc):
        dd, tt = place(px, py, pz, pc)
        return jnp.logical_and(dd == d, tt == t)

    def send(src, dst, ss, rs, to):
        return pltpu.make_async_remote_copy(
            src_ref=src, dst_ref=dst, send_sem=ss, recv_sem=rs, device_id=to, device_id_type=MESH
        )

    dest_a = [(lax.div(y, 2), 2 * x + core, 2 * m + y_odd, y_odd) for m in range(4)]
    dest_b = [(n, 2 * x + core, z, 1 - z_odd) for n in range(4)]
    row_block = 2 * x + core
    by_y_first = lax.rem(row_block + z, 2) == 0
    sources = [
        (
            lax.div(y, 2),
            jnp.where(by_y_first, row_block, s),
            jnp.where(by_y_first, s, z),
            y_odd,
        )
        for s in range(8)
    ]

    barrier = pltpu.get_barrier_semaphore()

    def greet(to):
        pl.semaphore_signal(barrier, inc=1, device_id=to, device_id_type=MESH)

    for o in range(1, 8):
        greet((d, lax.rem(t + o, 8)))
    for o in range(4):
        greet((d_core, lax.rem(x + o, 4) * 2 + zh))
    for o in range(1, 8):
        greet(place(x, lax.rem(y + o, 8), z, core))
        if o != 4:
            greet(place(x, y, lax.rem(z + o, 8), core))
    for source in sources:
        @pl.when(jnp.logical_not(mine(*source)))
        def _():
            greet(place(*source))
    expected = 24
    for dest in dest_a + dest_b:
        expected = expected + jnp.where(mine(*dest), 0, 1)
    pl.semaphore_wait(barrier, expected)

    k_out, q_out, g_out, own = [], [], [], []
    for j in range(2):
        def cols(head_x, per_x, width):
            return pl.ds(pl.multiple_of(head_x * per_x + j * width, 128), width)

        k_row, q_row, g_row = [], [], []
        for o in (4, 2, 6, 1, 7, 3, 5):
            to = lax.rem(t + o, 8)
            k_row.append(send(
                k_ref.at[0, :, cols(lax.div(to, 2), 256, 128)], kb.at[j, t],
                k_ss.at[j, o - 1], k_rs.at[j, o - 1], (d, to),
            ))
        for o in (2, 1, 3):
            tx = lax.rem(x + o, 4)
            q_row.append(send(
                q_ref.at[0, :, cols(tx, 1280, 640)], qb.at[j, x],
                q_ss.at[j, o - 1], q_rs.at[j, o - 1], (d, tx * 2 + zh),
            ))
            g_row.append(send(
                g_ref.at[0, :, cols(tx, 1280, 640)], gb.at[j, x],
                g_ss.at[j, o - 1], g_rs.at[j, o - 1], (d, tx * 2 + zh),
            ))
        own_row = [
            pltpu.make_async_copy(k_ref.at[0, :, cols(x, 256, 128)], kb.at[j, t], own_sem.at[j, 0]),
            pltpu.make_async_copy(q_ref.at[0, :, cols(x, 1280, 640)], qb.at[j, x], own_sem.at[j, 1]),
            pltpu.make_async_copy(g_ref.at[0, :, cols(x, 1280, 640)], gb.at[j, x], own_sem.at[j, 2]),
        ]
        for copy in k_row + q_row + g_row + own_row:
            copy.start()
        k_out.append(k_row)
        q_out.append(q_row)
        g_out.append(g_row)
        own.append(own_row)

    key_pos = lax.broadcasted_iota(jnp.int32, (128, 128), 0)
    query_pos = lax.broadcasted_iota(jnp.int32, (128, 128), 1)
    for k in range(4):
        for c in range(2 * k + 2):
            seen = jnp.where(mask_ref[0, 2 * k + zh, c] == 1, 0.0, HIDDEN)
            behind = key_pos + c * 128 <= query_pos + (2 * k + zh) * 128
            bias[k, c * 128 : (c + 1) * 128] = jnp.where(behind, seen, HIDDEN)
    vacc[...] = jnp.zeros_like(vacc)

    scale = math.log2(math.e) / math.sqrt(HEAD)

    def attend(j):
        for k in range(4):
            n = (2 * k + 2) * 128
            keys = kb[j, 0 : 2 * k + 2].reshape(n, 128)

            @pl.loop(0, GROUP)
            def _(h):
                col = pl.ds(pl.multiple_of(h * 128, 128), 128)
                s = lax.dot_general(
                    keys, qb[j, k, :, col], (((1,), (1,)), ((), ())), preferred_element_type=F32
                )
                s = s * scale + bias[k, 0:n]
                p = jnp.exp2(s - jnp.max(s, axis=0, keepdims=True))
                w = (p * (1.0 / jnp.sum(p, axis=0, keepdims=True))).astype(BF16)
                vacc[j, 0:n] += jnp.dot(w, gb[j, k, :, col], preferred_element_type=F32)

    z_out, x_out = [], []
    for j in range(2):
        for copy in k_out[j] + q_out[j] + g_out[j]:
            copy.wait_recv()
        for copy in own[j]:
            copy.wait()
        if j == 0:
            for o in (4, 2, 6, 5, 3, 7, 1):
                tx, tc = lax.rem(x + o // 2, 4), lax.rem(core + o % 2, 2)
                x_out.append(send(
                    x_ref.at[0, :, pl.ds(pl.multiple_of(tx * 1280 + tc * 640, 128), 640)],
                    xb.at[core, x], x_ss.at[o - 1], x_rs.at[o - 1], (d - core + tc, tx * 2 + zh),
                ))
            own_x = pltpu.make_async_copy(
                x_ref.at[0, :, pl.ds(pl.multiple_of(x * 1280 + core * 640, 128), 640)],
                xb.at[core, x], own_sem.at[0, 3],
            )
            for copy in x_out + [own_x]:
                copy.start()
        attend(j)
        for k in range(4):
            far = pl.ds(pl.multiple_of((2 * k + 1 - zh) * 128, 128), 128)
            vsend[j, k * 128 : (k + 1) * 128] = vacc[j, far].astype(BF16)
        z_out.append(send(
            vsend.at[j], vrecv.at[j], z_ss.at[j], z_rs.at[j], (d, x * 2 + 1 - zh)
        ))
        z_out[j].start()

    a_out = []
    for j in range(2):
        z_out[j].wait_recv()
        for k in range(4):
            near = pl.ds(pl.multiple_of((2 * k + zh) * 128, 128), 128)
            rows = pl.ds(k * 128, 128)
            v2[core, 2 * x + j, rows] = (vacc[j, near] + vrecv[j, rows].astype(F32)).astype(BF16)
        mine_v = v2.at[core, 2 * x + j]
        row = []
        for o in (2, 1, 3):
            row.append(send(
                mine_v, mine_v, a_ss.at[j, o], a_rs.at[j, o], (d, lax.rem(x + o, 4) * 2 + zh)
            ))
        row.append(send(mine_v, mine_v, f_ss.at[j, 0], f_rs.at[j, 0], (d_core, t)))
        for copy in row:
            copy.start()
        a_out.append(row)

    for copy in x_out:
        copy.wait_recv()
    own_x.wait()
    for i in range(8):
        xt[:, i * 128 : (i + 1) * 128] = jnp.transpose(xb[i // 4, i % 4])

    f_out = []
    for j in range(2):
        for o, copy in zip((2, 1, 3), a_out[j]):
            copy.wait_recv()
            block = v2.at[core, 2 * lax.rem(x + 4 - o, 4) + j]
            f_out.append(send(block, block, f_ss.at[j, o], f_rs.at[j, o], (d_core, t)))
            f_out[-1].start()
    for g in range(8):
        vgrad_ref[0, :, g * 128 : (g + 1) * 128] = v2[core, g, pl.ds(pl.multiple_of(x * 128, 128), 128)]
    for copy in f_out + [row[3] for row in a_out]:
        copy.wait_recv()

    @pl.loop(0, 4)
    def _(xx):
        for zz in range(4):
            rows = slice(zz * 160, (zz + 1) * 160)
            total = jnp.zeros((160, 256), F32)
            for cs in range(2):
                values = jnp.concatenate([v2[cs, 2 * xx], v2[cs, 2 * xx + 1]], axis=1)
                total += jnp.dot(
                    xt[rows, cs * 512 : (cs + 1) * 512], values, preferred_element_type=F32
                )
            total = total.astype(BF16)
            for cc in range(2):
                for hh in range(2):
                    block = total[cc * 80 : (cc + 1) * 80, hh * 128 : (hh + 1) * 128]
                    if (cc + zz) % 2 == 0:
                        ca[2 * xx + cc, hh * 2 + zz // 2] = block
                    else:
                        cb[hh * 4 + zz, xx] = block

    ra_out, rb_out = [], []
    for o in (4, 3, 5, 2, 6, 1, 7):
        ty, tz = lax.rem(y + o, 8), lax.rem(z + o, 8)
        ra_out.append(send(
            ca.at[ty], ra.at[y], ra_ss.at[o - 1], ra_rs.at[o - 1], place(x, ty, z, core)
        ))
        rb_out.append(send(
            cb.at[tz], rb.at[z], rb_ss.at[o - 1], rb_rs.at[o - 1], place(x, y, tz, core)
        ))
        ra_out[-1].start()
        rb_out[-1].start()
    for copy in ra_out + rb_out:
        copy.wait_recv()
    for own_part, parts, me, out in ((ca, ra, y, sa), (cb, rb, z, sb)):
        for m in range(4):
            total = own_part[me, m].astype(F32)
            for o in range(1, 8):
                total += parts[lax.rem(me + o, 8), m].astype(F32)
            out[m] = total.astype(BF16)

    fin_out = []
    for i, dest in enumerate(dest_a + dest_b):
        src = (sa if i < 4 else sb).at[i % 4]
        slot = z if i < 4 else y
        copy = send(src, fin.at[slot], fin_ss.at[i], fin_rs.at[slot], place(*dest))
        fin_out.append((copy, dest))
        here = mine(*dest)

        @pl.when(here)
        def _():
            fin[slot] = src[...]

        @pl.when(jnp.logical_not(here))
        def _():
            copy.start()

    total = jnp.zeros((80, 128), F32)
    for s, source in enumerate(sources):
        @pl.when(jnp.logical_not(mine(*source)))
        def _():
            send(sa.at[0], fin.at[s], fin_ss.at[0], fin_rs.at[s], place(*source)).wait_recv()

        total += fin[s].astype(F32)
    wgrad_ref[...] = total * (1.0 / 64.0)

    for j in range(2):
        for copy in k_out[j] + q_out[j] + g_out[j] + a_out[j]:
            copy.wait_send()
    for copy in x_out + z_out + f_out + ra_out + rb_out:
        copy.wait_send()
    for copy, dest in fin_out:
        @pl.when(jnp.logical_not(mine(*dest)))
        def _():
            copy.wait_send()


def body(query_states, key_states, out_grad, layer_input, block_mask):
    vmem, dma = pltpu.VMEM, pltpu.SemaphoreType.DMA
    return pl.pallas_call(
        kernel,
        out_shape=(
            jax.ShapeDtypeStruct((1, 128, 1024), BF16),
            jax.ShapeDtypeStruct((80, 128), F32),
        ),
        in_specs=[pl.BlockSpec(memory_space=pl.ANY)] * 4 + [pl.BlockSpec(memory_space=pltpu.SMEM)],
        out_specs=(pl.BlockSpec(memory_space=vmem), pl.BlockSpec(memory_space=vmem)),
        scratch_shapes=[
            vmem((2, 4, 128, 640), BF16),
            vmem((2, 4, 128, 640), BF16),
            vmem((2, 8, 128, 128), BF16),
            vmem((2, 4, 128, 640), BF16),
            vmem((640, 1024), BF16),
            vmem((4, 1024, 128), F32),
            vmem((2, 1024, 128), F32),
            vmem((2, 512, 128), BF16),
            vmem((2, 512, 128), BF16),
            vmem((2, 8, 512, 128), BF16),
            vmem((8, 4, 80, 128), BF16),
            vmem((8, 4, 80, 128), BF16),
            vmem((8, 4, 80, 128), BF16),
            vmem((8, 4, 80, 128), BF16),
            vmem((4, 80, 128), BF16),
            vmem((4, 80, 128), BF16),
            vmem((8, 80, 128), BF16),
            dma((2, 4)),
            dma((2, 7)), dma((2, 7)), dma((2, 3)), dma((2, 3)), dma((2, 3)), dma((2, 3)),
            dma((7,)), dma((7,)), dma((2,)), dma((2,)), dma((2, 4)), dma((2, 4)),
            dma((2, 4)), dma((2, 4)), dma((7,)), dma((7,)), dma((7,)), dma((7,)),
            dma((8,)), dma((8,)),
        ],
        compiler_params=pltpu.CompilerParams(
            collective_id=0, has_side_effects=True, vmem_limit_bytes=48 * 2**20
        ),
        name="value_path",
    )(query_states, key_states, out_grad, layer_input, block_mask)


def solution(mesh):
    in_specs = (
        P("dp", "ctx", None),
        P("dp", "ctx", None),
        P("dp", "ctx", None),
        P("dp", "ctx", None),
        P("dp", None, None),
    )
    out_specs = (P("dp", "ctx", None), P("dp", "ctx"))
    return jax.shard_map(body, mesh=mesh, in_specs=in_specs, out_specs=out_specs, check_vma=False)
```

```python
import functools
import math

import jax
import jax.numpy as jnp
from jax import lax
from jax.experimental import pallas as pl
from jax.experimental.pallas import tpu as pltpu
from jax.sharding import PartitionSpec as P

HEAD = 128
GROUP = 5
BF16 = jnp.bfloat16
F32 = jnp.float32
MESH = pl.DeviceIdType.MESH
HIDDEN = -1e30
X_AT = 8
SHARE_AT = 8
AHEAD = 3


def kernel(
    q_ref, k_ref, g_ref, x_ref, mask_ref, vgrad_ref, parts_ref,
    qb, gb, kb, xin, xtl, xt, bias, vacc, vsend, vrecv, v2, ca, cb, ra, rb, sa, sb, fin,
    own_sem, q_own, g_own, k_ss, k_rs, q_ss, q_rs, g_ss, g_rs, x_ss, x_rs, z_ss, z_rs, a_ss, a_rs,
    f_ss, f_rs, ra_ss, ra_rs, rb_ss, rb_rs, fin_ss, fin_rs,
):
    d = lax.axis_index("dp")
    t = lax.axis_index("ctx")
    core = lax.rem(d, 2)
    zl = lax.rem(lax.div(d, 2), 4)
    y = lax.div(d, 8)
    x = lax.div(t, 2)
    zh = lax.rem(t, 2)
    z = zh * 4 + zl
    d_core = d + 1 - 2 * core
    y_odd = lax.rem(y, 2)
    zl_odd = lax.rem(zl, 2)

    def place(px, py, pz, pc):
        return ((py * 4 + lax.rem(pz, 4)) * 2 + pc, px * 2 + lax.div(pz, 4))

    def mine(px, py, pz, pc):
        dd, tt = place(px, py, pz, pc)
        return jnp.logical_and(dd == d, tt == t)

    def send(src, dst, ss, rs, to):
        return pltpu.make_async_remote_copy(
            src_ref=src, dst_ref=dst, send_sem=ss, recv_sem=rs, device_id=to, device_id_type=MESH
        )

    x_in = pltpu.make_async_copy(x_ref.at[0], xin, own_sem.at[0, 3])
    x_in.start()

    dest = []
    for j in range(2):
        for m in range(2):
            dest.append((2 * m + y_odd, y, j * 4 + x, core))
        for n in range(2):
            dest.append((zl, 4 * zh + 2 * n + 1 - zl_odd, j * 4 + x, core))
    y_first = lax.rem(x + y, 2) == 0
    half_z = lax.div(y, 4) * 4 + x
    sources = [
        (zl, jnp.where(y_first, y, s), jnp.where(y_first, s, half_z), core) for s in range(8)
    ]

    sent, open_recv = [], []

    def go(*copies):
        for copy in copies:
            copy.start()
            sent.append(copy)
            open_recv.append(copy)

    def arrive(*copies):
        for copy in copies:
            copy.wait_recv()
            open_recv[:] = [other for other in open_recv if other is not copy]

    def finish():
        for copy in open_recv:
            copy.wait_recv()
        for copy in sent:
            copy.wait_send()

    barrier = pltpu.get_barrier_semaphore()

    def greet(to):
        pl.semaphore_signal(barrier, inc=1, device_id=to, device_id_type=MESH)

    for o in range(1, 8):
        greet((d, lax.rem(t + o, 8)))
    for o in range(4):
        greet((d_core, lax.rem(x + o, 4) * 2 + zh))
    for o in range(1, 8):
        greet(place(x, lax.rem(y + o, 8), z, core))
        if o != 4:
            greet(place(x, y, lax.rem(z + o, 8), core))
    for source in sources:
        @pl.when(jnp.logical_not(mine(*source)))
        def _():
            greet(place(*source))
    expected = 24
    for to in dest:
        expected = expected + jnp.where(mine(*to), 0, 1)
    pl.semaphore_wait(barrier, expected)

    k_out = [[], []]

    def send_keys(j):
        for o in (4, 2, 6, 1, 7, 3, 5):
            to = lax.rem(t + o, 8)
            columns = pl.ds(pl.multiple_of(lax.div(to, 2) * 256 + j * 128, 128), 128)
            k_out[j].append(send(
                k_ref.at[0, :, columns], kb.at[j, t],
                k_ss.at[j, o - 1], k_rs.at[j, o - 1], (d, to),
            ))
        go(*k_out[j])
        columns = pl.ds(pl.multiple_of(x * 256 + j * 128, 128), 128)
        pltpu.make_async_copy(k_ref.at[0, :, columns], kb.at[j, t], own_sem.at[j, 0]).start()

    def head_sends(h):
        out = []
        for o in (2, 1, 3):
            tx = lax.rem(x + o, 4)
            columns = pl.ds(pl.multiple_of(tx * 1280 + h * 128, 128), 128)
            to = (d, tx * 2 + zh)
            out.append(send(q_ref.at[0, :, columns], qb.at[h, x], q_ss.at[h, o - 1], q_rs.at[h, o - 1], to))
            out.append(send(g_ref.at[0, :, columns], gb.at[h, x], g_ss.at[h, o - 1], g_rs.at[h, o - 1], to))
        return out

    def head_own(h):
        columns = pl.ds(pl.multiple_of(x * 1280 + h * 128, 128), 128)
        return [
            pltpu.make_async_copy(q_ref.at[0, :, columns], qb.at[h, x], q_own.at[h]),
            pltpu.make_async_copy(g_ref.at[0, :, columns], gb.at[h, x], g_own.at[h]),
        ]

    def send_head(h):
        for copy in head_sends(h) + head_own(h):
            copy.start()

    send_keys(0)
    pl.loop(0, AHEAD)(send_head)
    send_keys(1)

    key_pos = lax.broadcasted_iota(jnp.int32, (128, 128), 0)
    query_pos = lax.broadcasted_iota(jnp.int32, (128, 128), 1)
    for k in range(4):
        for c in range(2 * k + 2):
            seen = jnp.where(mask_ref[0, 2 * k + zh, c] == 1, 0.0, HIDDEN)
            behind = key_pos + c * 128 <= query_pos + (2 * k + zh) * 128
            bias[k, c * 128 : (c + 1) * 128] = jnp.where(behind, seen, HIDDEN)
    vacc[...] = jnp.zeros_like(vacc)

    scale = math.log2(math.e) / math.sqrt(HEAD)

    def attend(j, h):
        for k in range(4):
            n = (2 * k + 2) * 128
            keys = kb[j, 0 : 2 * k + 2].reshape(n, 128)
            s = lax.dot_general(
                keys, qb[h, k], (((1,), (1,)), ((), ())), preferred_element_type=F32
            )
            s = s * scale + bias[k, 0:n]
            p = jnp.exp2(s - jnp.max(s, axis=0, keepdims=True))
            w = (p * (1.0 / jnp.sum(p, axis=0, keepdims=True))).astype(BF16)
            vacc[j, 0:n] += jnp.dot(w, gb[h, k], preferred_element_type=F32)

    x_in.wait()

    @pl.loop(0, 8)
    def _(yy):
        turned = jnp.transpose(xin[:, pl.ds(pl.multiple_of(yy * 640, 128), 640)])
        for b in range(8):
            xtl[b, pl.ds(pl.multiple_of(yy * 80, 16), 80)] = turned[b * 80 : (b + 1) * 80]

    x_slot = xt.at[:, pl.ds(pl.multiple_of(core * 512 + x * 128, 128), 128)]
    own_x = pltpu.make_async_copy(xtl.at[x * 2 + core], x_slot, own_sem.at[1, 3])
    own_x.start()

    x_out = []
    for o in (4, 2, 6, 5, 3, 7, 1):
        tx, tc = lax.rem(x + o // 2, 4), lax.rem(core + o % 2, 2)
        x_out.append(send(
            xtl.at[tx * 2 + tc], x_slot,
            x_ss.at[o - 1], x_rs.at[o - 1], (d - core + tc, tx * 2 + zh),
        ))

    def send_x():
        for copy in x_out:
            copy.start()

    sent.extend(x_out)

    z_out = [
        send(vsend.at[j], vrecv.at[j], z_ss.at[j], z_rs.at[j], (d, x * 2 + 1 - zh)) for j in range(2)
    ]

    a_out, f_out = [[], []], [[], []]
    for j in range(2):
        mine_v = v2.at[core, 2 * x + j]
        for o in (2, 1, 3):
            a_out[j].append(send(
                mine_v, mine_v, a_ss.at[j, o], a_rs.at[j, o], (d, lax.rem(x + o, 4) * 2 + zh)
            ))
        f_out[j].append(send(mine_v, mine_v, f_ss.at[j, 0], f_rs.at[j, 0], (d_core, t)))

    def share(j):
        z_out[j].wait_recv()
        for k in range(4):
            near = pl.ds(pl.multiple_of((2 * k + zh) * 128, 128), 128)
            rows = pl.ds(k * 128, 128)
            v2[core, 2 * x + j, rows] = (vacc[j, near] + vrecv[j, rows].astype(F32)).astype(BF16)
        for copy in a_out[j] + f_out[j][:1]:
            copy.start()

    for j in range(2):
        arrive(*k_out[j])
        pltpu.make_async_copy(k_ref.at[0, :, 0:128], kb.at[j, t], own_sem.at[j, 0]).wait()

        @pl.loop(j * GROUP, (j + 1) * GROUP)
        def _(h):
            for copy in head_sends(h):
                copy.wait_recv()
            for copy in head_own(h):
                copy.wait()

            @pl.when(h < 2 * GROUP - AHEAD)
            def _():
                send_head(h + AHEAD)

            if j == 1:
                @pl.when(h == SHARE_AT)
                def _():
                    share(0)

                @pl.when(h == X_AT)
                def _():
                    send_x()

            attend(j, h)

        for k in range(4):
            far = pl.ds(pl.multiple_of((2 * k + 1 - zh) * 128, 128), 128)
            vsend[j, k * 128 : (k + 1) * 128] = vacc[j, far].astype(BF16)
        z_out[j].start()

    def forward(j):
        for o, copy in zip((2, 1, 3), a_out[j]):
            copy.wait_recv()
            block = v2.at[core, 2 * lax.rem(x + 4 - o, 4) + j]
            f_out[j].append(send(block, block, f_ss.at[j, o], f_rs.at[j, o], (d_core, t)))
            f_out[j][-1].start()

    def multiply(j):
        for copy in f_out[j]:
            copy.wait_recv()

        @pl.loop(0, 2)
        def _(xx):
            for r in range(4):
                rows = slice(r * 160, (r + 1) * 160)
                total = jnp.zeros((160, 256), F32)
                for cs in range(2):
                    values = jnp.concatenate([v2[cs, 4 * xx + j], v2[cs, 4 * xx + 2 + j]], axis=1)
                    total += jnp.dot(
                        xt[rows, cs * 512 : (cs + 1) * 512], values, preferred_element_type=F32
                    )
                total = total.astype(BF16)
                for cc in range(2):
                    for hh in range(2):
                        block = total[cc * 80 : (cc + 1) * 80, hh * 128 : (hh + 1) * 128]
                        if cc == hh:
                            ca[j, 2 * r + cc, xx] = block
                        else:
                            cb[j, (r // 2) * 4 + 2 * xx + hh, r % 2] = block

    ra_out, rb_out = [[], []], [[], []]

    def first_sum(j):
        for o in (4, 3, 5, 2, 6, 1, 7):
            ty, tz = lax.rem(y + o, 8), lax.rem(z + o, 8)
            ra_out[j].append(send(
                ca.at[j, ty], ra.at[j, y], ra_ss.at[j, o - 1], ra_rs.at[j, o - 1],
                place(x, ty, z, core),
            ))
            rb_out[j].append(send(
                cb.at[j, tz], rb.at[j, z], rb_ss.at[j, o - 1], rb_rs.at[j, o - 1],
                place(x, y, tz, core),
            ))
            go(ra_out[j][-1], rb_out[j][-1])

    fin_out = []

    def second_sum(j):
        arrive(*ra_out[j], *rb_out[j])
        for own_part, parts, me, out in ((ca, ra, y, sa), (cb, rb, z, sb)):
            for m in range(2):
                total = own_part[j, me, m].astype(F32)
                for o in range(1, 8):
                    total += parts[j, lax.rem(me + o, 8), m].astype(F32)
                out[j, m] = total.astype(BF16)
        for i in range(4):
            src = (sa if i < 2 else sb).at[j, i % 2]
            slot = z if i < 2 else y
            to = dest[j * 4 + i]
            copy = send(src, fin.at[slot], fin_ss.at[j * 4 + i], fin_rs.at[slot], place(*to))
            fin_out.append((copy, to))
            here = mine(*to)

            @pl.when(here)
            def _():
                fin[slot] = src[...]

            @pl.when(jnp.logical_not(here))
            def _():
                copy.start()

    forward(0)
    share(1)
    for copy in x_out:
        copy.wait_recv()
    own_x.wait()
    multiply(0)
    first_sum(0)
    forward(1)
    for g in range(8):
        vgrad_ref[0, :, g * 128 : (g + 1) * 128] = v2[core, g, pl.ds(pl.multiple_of(x * 128, 128), 128)]
    multiply(1)
    first_sum(1)
    second_sum(0)
    second_sum(1)

    for s, source in enumerate(sources):
        @pl.when(jnp.logical_not(mine(*source)))
        def _():
            send(sa.at[0, 0], fin.at[s], fin_ss.at[0], fin_rs.at[s], place(*source)).wait_recv()

        parts_ref[s] = fin[s]

    finish()
    for copy in z_out + a_out[0] + a_out[1] + f_out[0] + f_out[1]:
        copy.wait_send()

    @pl.loop(0, 2 * GROUP)
    def _(h):
        for copy in head_sends(h):
            copy.wait_send()

    for copy, to in fin_out:
        @pl.when(jnp.logical_not(mine(*to)))
        def _():
            copy.wait_send()


def add_parts(values_ref, parts_ref, vgrad_ref, wgrad_ref):
    vgrad_ref[...] = values_ref[...]
    total = parts_ref[0].astype(F32)
    for s in range(1, 8):
        total += parts_ref[s].astype(F32)
    wgrad_ref[...] = total * (1.0 / 64.0)


def body(query_states, key_states, out_grad, layer_input, block_mask):
    vmem, dma = pltpu.VMEM, pltpu.SemaphoreType.DMA
    values, parts = pl.pallas_call(
        kernel,
        out_shape=(
            jax.ShapeDtypeStruct((1, 128, 1024), BF16),
            jax.ShapeDtypeStruct((8, 80, 128), BF16),
        ),
        in_specs=[pl.BlockSpec(memory_space=pltpu.HBM)] * 4 + [pl.BlockSpec(memory_space=pltpu.SMEM)],
        out_specs=(pl.BlockSpec(memory_space=vmem), pl.BlockSpec(memory_space=vmem)),
        scratch_shapes=[
            vmem((10, 4, 128, 128), BF16),
            vmem((10, 4, 128, 128), BF16),
            vmem((2, 8, 128, 128), BF16),
            vmem((128, 5120), BF16),
            vmem((8, 640, 128), BF16),
            vmem((640, 1024), BF16),
            vmem((4, 1024, 128), F32),
            vmem((2, 1024, 128), F32),
            vmem((2, 512, 128), BF16),
            vmem((2, 512, 128), BF16),
            vmem((2, 8, 512, 128), BF16),
            vmem((2, 8, 2, 80, 128), BF16),
            vmem((2, 8, 2, 80, 128), BF16),
            vmem((2, 8, 2, 80, 128), BF16),
            vmem((2, 8, 2, 80, 128), BF16),
            vmem((2, 2, 80, 128), BF16),
            vmem((2, 2, 80, 128), BF16),
            vmem((8, 80, 128), BF16),
            dma((2, 4)),
            dma((10,)), dma((10,)),
            dma((2, 7)), dma((2, 7)), dma((10, 3)), dma((10, 3)), dma((10, 3)), dma((10, 3)),
            dma((7,)), dma((7,)), dma((2,)), dma((2,)), dma((2, 4)), dma((2, 4)),
            dma((2, 4)), dma((2, 4)), dma((2, 7)), dma((2, 7)), dma((2, 7)), dma((2, 7)),
            dma((8,)), dma((8,)),
        ],
        compiler_params=pltpu.CompilerParams(
            collective_id=0, has_side_effects=True, vmem_limit_bytes=60 * 2**20
        ),
        name="value_path",
    )(query_states, key_states, out_grad, layer_input, block_mask)
    return pl.pallas_call(
        add_parts,
        out_shape=(
            jax.ShapeDtypeStruct((1, 128, 1024), BF16),
            jax.ShapeDtypeStruct((80, 128), F32),
        ),
        name="add_parts",
    )(values, parts)


def solution(mesh):
    in_specs = (
        P("dp", "ctx", None),
        P("dp", "ctx", None),
        P("dp", "ctx", None),
        P("dp", "ctx", None),
        P("dp", None, None),
    )
    out_specs = (P("dp", "ctx", None), P("dp", "ctx"))
    return jax.shard_map(body, mesh=mesh, in_specs=in_specs, out_specs=out_specs, check_vma=False)
```

```python
import functools
import math

import jax
import jax.numpy as jnp
from jax import lax
from jax.experimental import pallas as pl
from jax.experimental.pallas import tpu as pltpu
from jax.sharding import PartitionSpec as P

HEAD = 128
GROUP = 5
BF16 = jnp.bfloat16
F32 = jnp.float32
MESH = pl.DeviceIdType.MESH
HIDDEN = -1e30
X_AT = 8
SHARE_AT = 8
AHEAD = 5


def kernel(
    q_ref, k_ref, g_ref, x_ref, mask_ref, vgrad_ref, parts_ref,
    qb, gb, kb, xin, xtl, xt, bias, vacc, vsend, vrecv, v2, ca, cb, ra, rb, sa, sb, fin,
    ring_sem, z_sem, y_sem, core_sem, own_sem, q_own, g_own, k_ss, k_rs, q_ss, q_rs, g_ss, g_rs, x_ss, x_rs, z_ss, z_rs, a_ss, a_rs,
    f_ss, f_rs, ra_ss, ra_rs, rb_ss, rb_rs, fin_ss, fin_rs,
):
    d = lax.axis_index("dp")
    t = lax.axis_index("ctx")
    core = lax.rem(d, 2)
    zl = lax.rem(lax.div(d, 2), 4)
    y = lax.div(d, 8)
    x = lax.div(t, 2)
    zh = lax.rem(t, 2)
    z = zh * 4 + zl
    d_core = d + 1 - 2 * core
    y_odd = lax.rem(y, 2)
    zl_odd = lax.rem(zl, 2)

    def place(px, py, pz, pc):
        return ((py * 4 + lax.rem(pz, 4)) * 2 + pc, px * 2 + lax.div(pz, 4))

    def mine(px, py, pz, pc):
        dd, tt = place(px, py, pz, pc)
        return jnp.logical_and(dd == d, tt == t)

    def send(src, dst, ss, rs, to):
        return pltpu.make_async_remote_copy(
            src_ref=src, dst_ref=dst, send_sem=ss, recv_sem=rs, device_id=to, device_id_type=MESH
        )

    x_in = pltpu.make_async_copy(x_ref.at[0], xin, own_sem.at[0, 3])
    x_in.start()

    dest = []
    for j in range(2):
        for m in range(2):
            dest.append((2 * m + y_odd, y, j * 4 + x, core))
        for n in range(2):
            dest.append((zl, 4 * zh + 2 * n + 1 - zl_odd, j * 4 + x, core))
    y_first = lax.rem(x + y, 2) == 0
    half_z = lax.div(y, 4) * 4 + x
    sources = [
        (zl, jnp.where(y_first, y, s), jnp.where(y_first, s, half_z), core) for s in range(8)
    ]

    sent, open_recv = [], []

    def go(*copies):
        for copy in copies:
            copy.start()
            sent.append(copy)
            open_recv.append(copy)

    def arrive(*copies):
        for copy in copies:
            copy.wait_recv()
            open_recv[:] = [other for other in open_recv if other is not copy]

    def finish():
        for copy in open_recv:
            copy.wait_recv()
        for copy in sent:
            copy.wait_send()

    barrier = pltpu.get_barrier_semaphore()

    def greet(to):
        pl.semaphore_signal(barrier, inc=1, device_id=to, device_id_type=MESH)

    def tell(sem, px):
        pl.semaphore_signal(sem, inc=1, device_id=(d, px * 2 + zh), device_id_type=MESH)

    @pl.when(x != 2)
    def _():
        greet((d, 4 + zh))

    @pl.when(x == 2)
    def _():
        pl.semaphore_wait(barrier, 3)
        for px in (0, 1, 3):
            tell(ring_sem, px)

    @pl.when(x != 2)
    def _():
        pl.semaphore_wait(ring_sem, 1)

    def meet_z():
        @pl.when(x == 0)
        def _():
            for o in range(1, 8):
                greet(place(0, y, lax.rem(z + o, 8), core))
            pl.semaphore_wait(barrier, 7)
            for px in (1, 2, 3):
                tell(z_sem, px)

        @pl.when(x != 0)
        def _():
            pl.semaphore_wait(z_sem, 1)

        @pl.when(x == 1)
        def _():
            for o in range(1, 8):
                greet(place(1, lax.rem(y + o, 8), z, core))

        @pl.when(x == 3)
        def _():
            greet((d_core, t))

    def meet_rest():
        @pl.when(x == 1)
        def _():
            pl.semaphore_wait(barrier, 7)
            for px in (0, 2, 3):
                tell(y_sem, px)

        @pl.when(x == 3)
        def _():
            pl.semaphore_wait(barrier, 1)
            for px in (0, 1, 2):
                tell(core_sem, px)

        @pl.when(x != 1)
        def _():
            pl.semaphore_wait(y_sem, 1)

        @pl.when(x != 3)
        def _():
            pl.semaphore_wait(core_sem, 1)

    k_out = [[], []]

    def send_keys(j, far):
        new = []
        for o in (0, 2, 1, 3) if far else (2, 1, 3):
            tx = lax.rem(x + o, 4)
            columns = pl.ds(pl.multiple_of(tx * 256 + j * 128, 128), 128)
            i = o - 1 + 4 * far
            new.append(send(
                k_ref.at[0, :, columns], kb.at[j, t], k_ss.at[j, i], k_rs.at[j, i],
                (d, tx * 2 + (1 - zh if far else zh)),
            ))
        k_out[j].extend(new)
        go(*new)
        if far:
            return
        columns = pl.ds(pl.multiple_of(x * 256 + j * 128, 128), 128)
        pltpu.make_async_copy(k_ref.at[0, :, columns], kb.at[j, t], own_sem.at[j, 0]).start()

    def head_sends(h):
        out = []
        for o in (2, 1, 3):
            tx = lax.rem(x + o, 4)
            columns = pl.ds(pl.multiple_of(tx * 1280 + h * 128, 128), 128)
            to = (d, tx * 2 + zh)
            out.append(send(q_ref.at[0, :, columns], qb.at[h, x], q_ss.at[h, o - 1], q_rs.at[h, o - 1], to))
            out.append(send(g_ref.at[0, :, columns], gb.at[h, x], g_ss.at[h, o - 1], g_rs.at[h, o - 1], to))
        return out

    def head_own(h):
        columns = pl.ds(pl.multiple_of(x * 1280 + h * 128, 128), 128)
        return [
            pltpu.make_async_copy(q_ref.at[0, :, columns], qb.at[h, x], q_own.at[h]),
            pltpu.make_async_copy(g_ref.at[0, :, columns], gb.at[h, x], g_own.at[h]),
        ]

    def send_head(h):
        for copy in head_sends(h) + head_own(h):
            copy.start()

    send_keys(0, False)
    pl.loop(0, AHEAD)(send_head)
    send_keys(1, False)
    meet_z()
    send_keys(0, True)
    send_keys(1, True)

    key_pos = lax.broadcasted_iota(jnp.int32, (128, 128), 0)
    query_pos = lax.broadcasted_iota(jnp.int32, (128, 128), 1)
    for k in range(4):
        for c in range(2 * k + 2):
            seen = jnp.where(mask_ref[0, 2 * k + zh, c] == 1, 0.0, HIDDEN)
            behind = key_pos + c * 128 <= query_pos + (2 * k + zh) * 128
            bias[k, c * 128 : (c + 1) * 128] = jnp.where(behind, seen, HIDDEN)
    vacc[...] = jnp.zeros_like(vacc)

    scale = math.log2(math.e) / math.sqrt(HEAD)

    def attend(j, h):
        for k in range(4):
            n = (2 * k + 2) * 128
            keys = kb[j, 0 : 2 * k + 2].reshape(n, 128)
            s = lax.dot_general(
                keys, qb[h, k], (((1,), (1,)), ((), ())), preferred_element_type=F32
            )
            s = s * scale + bias[k, 0:n]
            p = jnp.exp2(s - jnp.max(s, axis=0, keepdims=True))
            w = (p * (1.0 / jnp.sum(p, axis=0, keepdims=True))).astype(BF16)
            vacc[j, 0:n] += jnp.dot(w, gb[h, k], preferred_element_type=F32)

    x_in.wait()

    @pl.loop(0, 8)
    def _(yy):
        turned = jnp.transpose(xin[:, pl.ds(pl.multiple_of(yy * 640, 128), 640)])
        for b in range(8):
            xtl[b, pl.ds(pl.multiple_of(yy * 80, 16), 80)] = turned[b * 80 : (b + 1) * 80]

    x_slot = xt.at[:, pl.ds(pl.multiple_of(core * 512 + x * 128, 128), 128)]
    own_x = pltpu.make_async_copy(xtl.at[x * 2 + core], x_slot, own_sem.at[1, 3])
    own_x.start()

    x_out = []
    for o in (4, 2, 6, 5, 3, 7, 1):
        tx, tc = lax.rem(x + o // 2, 4), lax.rem(core + o % 2, 2)
        x_out.append(send(
            xtl.at[tx * 2 + tc], x_slot,
            x_ss.at[o - 1], x_rs.at[o - 1], (d - core + tc, tx * 2 + zh),
        ))

    def send_x():
        for copy in x_out:
            copy.start()

    sent.extend(x_out)

    z_out = [
        send(vsend.at[j], vrecv.at[j], z_ss.at[j], z_rs.at[j], (d, x * 2 + 1 - zh)) for j in range(2)
    ]

    a_out, f_out = [[], []], [[], []]
    for j in range(2):
        mine_v = v2.at[core, 2 * x + j]
        for o in (2, 1, 3):
            a_out[j].append(send(
                mine_v, mine_v, a_ss.at[j, o], a_rs.at[j, o], (d, lax.rem(x + o, 4) * 2 + zh)
            ))
        f_out[j].append(send(mine_v, mine_v, f_ss.at[j, 0], f_rs.at[j, 0], (d_core, t)))

    def share(j):
        z_out[j].wait_recv()
        for k in range(4):
            near = pl.ds(pl.multiple_of((2 * k + zh) * 128, 128), 128)
            rows = pl.ds(k * 128, 128)
            v2[core, 2 * x + j, rows] = (vacc[j, near] + vrecv[j, rows].astype(F32)).astype(BF16)
        for copy in a_out[j] + f_out[j][:1]:
            copy.start()

    for j in range(2):
        arrive(*k_out[j])
        pltpu.make_async_copy(k_ref.at[0, :, 0:128], kb.at[j, t], own_sem.at[j, 0]).wait()

        @pl.loop(j * GROUP, (j + 1) * GROUP)
        def _(h):
            for copy in head_sends(h):
                copy.wait_recv()
            for copy in head_own(h):
                copy.wait()

            @pl.when(h < 2 * GROUP - AHEAD)
            def _():
                send_head(h + AHEAD)

            if j == 1:
                @pl.when(h == GROUP)
                def _():
                    meet_rest()

                @pl.when(h == SHARE_AT)
                def _():
                    share(0)

                @pl.when(h == X_AT)
                def _():
                    send_x()

            attend(j, h)

        for k in range(4):
            far = pl.ds(pl.multiple_of((2 * k + 1 - zh) * 128, 128), 128)
            vsend[j, k * 128 : (k + 1) * 128] = vacc[j, far].astype(BF16)
        z_out[j].start()

    def forward(j):
        for o, copy in zip((2, 1, 3), a_out[j]):
            copy.wait_recv()
            block = v2.at[core, 2 * lax.rem(x + 4 - o, 4) + j]
            f_out[j].append(send(block, block, f_ss.at[j, o], f_rs.at[j, o], (d_core, t)))
            f_out[j][-1].start()

    def multiply(j):
        for copy in f_out[j]:
            copy.wait_recv()

        @pl.loop(0, 2)
        def _(xx):
            for r in range(4):
                rows = slice(r * 160, (r + 1) * 160)
                total = jnp.zeros((160, 256), F32)
                for cs in range(2):
                    values = jnp.concatenate([v2[cs, 4 * xx + j], v2[cs, 4 * xx + 2 + j]], axis=1)
                    total += jnp.dot(
                        xt[rows, cs * 512 : (cs + 1) * 512], values, preferred_element_type=F32
                    )
                total = total.astype(BF16)
                for cc in range(2):
                    for hh in range(2):
                        block = total[cc * 80 : (cc + 1) * 80, hh * 128 : (hh + 1) * 128]
                        if cc == hh:
                            ca[j, 2 * r + cc, xx] = block
                        else:
                            cb[j, (r // 2) * 4 + 2 * xx + hh, r % 2] = block

    ra_out, rb_out = [[], []], [[], []]

    def first_sum(j):
        for o in (4, 3, 5, 2, 6, 1, 7):
            ty, tz = lax.rem(y + o, 8), lax.rem(z + o, 8)
            ra_out[j].append(send(
                ca.at[j, ty], ra.at[j, y], ra_ss.at[j, o - 1], ra_rs.at[j, o - 1],
                place(x, ty, z, core),
            ))
            rb_out[j].append(send(
                cb.at[j, tz], rb.at[j, z], rb_ss.at[j, o - 1], rb_rs.at[j, o - 1],
                place(x, y, tz, core),
            ))
            go(ra_out[j][-1], rb_out[j][-1])

    fin_out = []

    def second_sum(j):
        arrive(*ra_out[j], *rb_out[j])
        for own_part, parts, me, out in ((ca, ra, y, sa), (cb, rb, z, sb)):
            for m in range(2):
                total = own_part[j, me, m].astype(F32)
                for o in range(1, 8):
                    total += parts[j, lax.rem(me + o, 8), m].astype(F32)
                out[j, m] = total.astype(BF16)
        for i in range(4):
            src = (sa if i < 2 else sb).at[j, i % 2]
            slot = z if i < 2 else y
            to = dest[j * 4 + i]
            copy = send(src, fin.at[slot], fin_ss.at[j * 4 + i], fin_rs.at[slot], place(*to))
            fin_out.append((copy, to))
            here = mine(*to)

            @pl.when(here)
            def _():
                fin[slot] = src[...]

            @pl.when(jnp.logical_not(here))
            def _():
                copy.start()

    forward(0)
    share(1)
    for copy in x_out:
        copy.wait_recv()
    own_x.wait()
    multiply(0)
    first_sum(0)
    forward(1)
    for g in range(8):
        vgrad_ref[0, :, g * 128 : (g + 1) * 128] = v2[core, g, pl.ds(pl.multiple_of(x * 128, 128), 128)]
    multiply(1)
    first_sum(1)
    second_sum(0)
    second_sum(1)

    for s, source in enumerate(sources):
        @pl.when(jnp.logical_not(mine(*source)))
        def _():
            send(sa.at[0, 0], fin.at[s], fin_ss.at[0], fin_rs.at[s], place(*source)).wait_recv()

        parts_ref[s] = fin[s]

    finish()
    for copy in z_out + a_out[0] + a_out[1] + f_out[0] + f_out[1]:
        copy.wait_send()

    @pl.loop(0, 2 * GROUP)
    def _(h):
        for copy in head_sends(h):
            copy.wait_send()

    for copy, to in fin_out:
        @pl.when(jnp.logical_not(mine(*to)))
        def _():
            copy.wait_send()


def add_parts(values_ref, parts_ref, vgrad_ref, wgrad_ref):
    vgrad_ref[...] = values_ref[...]
    total = parts_ref[0].astype(F32)
    for s in range(1, 8):
        total += parts_ref[s].astype(F32)
    wgrad_ref[...] = total * (1.0 / 64.0)


def body(query_states, key_states, out_grad, layer_input, block_mask):
    vmem, dma, regular = pltpu.VMEM, pltpu.SemaphoreType.DMA, pltpu.SemaphoreType.REGULAR
    values, parts = pl.pallas_call(
        kernel,
        out_shape=(
            jax.ShapeDtypeStruct((1, 128, 1024), BF16),
            jax.ShapeDtypeStruct((8, 80, 128), BF16),
        ),
        in_specs=[pl.BlockSpec(memory_space=pltpu.HBM)] * 4 + [pl.BlockSpec(memory_space=pltpu.SMEM)],
        out_specs=(pl.BlockSpec(memory_space=vmem), pl.BlockSpec(memory_space=vmem)),
        scratch_shapes=[
            vmem((10, 4, 128, 128), BF16),
            vmem((10, 4, 128, 128), BF16),
            vmem((2, 8, 128, 128), BF16),
            vmem((128, 5120), BF16),
            vmem((8, 640, 128), BF16),
            vmem((640, 1024), BF16),
            vmem((4, 1024, 128), F32),
            vmem((2, 1024, 128), F32),
            vmem((2, 512, 128), BF16),
            vmem((2, 512, 128), BF16),
            vmem((2, 8, 512, 128), BF16),
            vmem((2, 8, 2, 80, 128), BF16),
            vmem((2, 8, 2, 80, 128), BF16),
            vmem((2, 8, 2, 80, 128), BF16),
            vmem((2, 8, 2, 80, 128), BF16),
            vmem((2, 2, 80, 128), BF16),
            vmem((2, 2, 80, 128), BF16),
            vmem((8, 80, 128), BF16),
            regular, regular, regular, regular,
            dma((2, 4)),
            dma((10,)), dma((10,)),
            dma((2, 7)), dma((2, 7)), dma((10, 3)), dma((10, 3)), dma((10, 3)), dma((10, 3)),
            dma((7,)), dma((7,)), dma((2,)), dma((2,)), dma((2, 4)), dma((2, 4)),
            dma((2, 4)), dma((2, 4)), dma((2, 7)), dma((2, 7)), dma((2, 7)), dma((2, 7)),
            dma((8,)), dma((8,)),
        ],
        compiler_params=pltpu.CompilerParams(
            collective_id=0, has_side_effects=True, vmem_limit_bytes=60 * 2**20
        ),
        name="value_path",
    )(query_states, key_states, out_grad, layer_input, block_mask)
    return pl.pallas_call(
        add_parts,
        out_shape=(
            jax.ShapeDtypeStruct((1, 128, 1024), BF16),
            jax.ShapeDtypeStruct((80, 128), F32),
        ),
        name="add_parts",
    )(values, parts)


def solution(mesh):
    in_specs = (
        P("dp", "ctx", None),
        P("dp", "ctx", None),
        P("dp", "ctx", None),
        P("dp", "ctx", None),
        P("dp", None, None),
    )
    out_specs = (P("dp", "ctx", None), P("dp", "ctx"))
    return jax.shard_map(body, mesh=mesh, in_specs=in_specs, out_specs=out_specs, check_vma=False)
```

```python
import functools
import math

import jax
import jax.numpy as jnp
from jax import lax
from jax.experimental import pallas as pl
from jax.experimental.pallas import tpu as pltpu
from jax.sharding import PartitionSpec as P

HEAD = 128
GROUP = 5
BF16 = jnp.bfloat16
F32 = jnp.float32
MESH = pl.DeviceIdType.MESH
HIDDEN = -1e30
X_AT = 9
SHARE_AT = 8
AHEAD = 5


def kernel(
    q_ref, k_ref, g_ref, x_ref, mask_ref, vgrad_ref, parts_ref,
    qb, gb, kb, xin, xtl, xt, bias, vacc, vsend, vrecv, v2, ca, cb, ra, rb, sa, sb, fin,
    ring_sem, z_sem, y_sem, core_sem, own_sem, q_own, g_own, k_ss, k_rs, q_ss, q_rs, g_ss, g_rs, x_ss, x_rs, z_ss, z_rs, a_ss, a_rs,
    f_ss, f_rs, ra_ss, ra_rs, rb_ss, rb_rs, fin_ss, fin_rs,
):
    d = lax.axis_index("dp")
    t = lax.axis_index("ctx")
    core = lax.rem(d, 2)
    zl = lax.rem(lax.div(d, 2), 4)
    y = lax.div(d, 8)
    x = lax.div(t, 2)
    zh = lax.rem(t, 2)
    z = zh * 4 + zl
    d_core = d + 1 - 2 * core
    y_odd = lax.rem(y, 2)
    zl_odd = lax.rem(zl, 2)

    def place(px, py, pz, pc):
        return ((py * 4 + lax.rem(pz, 4)) * 2 + pc, px * 2 + lax.div(pz, 4))

    def mine(px, py, pz, pc):
        dd, tt = place(px, py, pz, pc)
        return jnp.logical_and(dd == d, tt == t)

    def send(src, dst, ss, rs, to):
        return pltpu.make_async_remote_copy(
            src_ref=src, dst_ref=dst, send_sem=ss, recv_sem=rs, device_id=to, device_id_type=MESH
        )

    x_in = pltpu.make_async_copy(x_ref.at[0], xin, own_sem.at[0, 3])
    x_in.start()

    dest = []
    for j in range(2):
        for m in range(2):
            dest.append((2 * m + y_odd, y, j * 4 + x, core))
        for n in range(2):
            dest.append((zl, 4 * zh + 2 * n + 1 - zl_odd, j * 4 + x, core))
    y_first = lax.rem(x + y, 2) == 0
    half_z = lax.div(y, 4) * 4 + x
    sources = [
        (zl, jnp.where(y_first, y, s), jnp.where(y_first, s, half_z), core) for s in range(8)
    ]

    sent, open_recv = [], []

    def go(*copies):
        for copy in copies:
            copy.start()
            sent.append(copy)
            open_recv.append(copy)

    def arrive(*copies):
        for copy in copies:
            copy.wait_recv()
            open_recv[:] = [other for other in open_recv if other is not copy]

    def finish():
        for copy in open_recv:
            copy.wait_recv()
        for copy in sent:
            copy.wait_send()

    barrier = pltpu.get_barrier_semaphore()

    def greet(to):
        pl.semaphore_signal(barrier, inc=1, device_id=to, device_id_type=MESH)

    def tell(sem, px):
        pl.semaphore_signal(sem, inc=1, device_id=(d, px * 2 + zh), device_id_type=MESH)

    @pl.when(x != 2)
    def _():
        greet((d, 4 + zh))

    @pl.when(x == 2)
    def _():
        pl.semaphore_wait(barrier, 3)
        for px in (0, 1, 3):
            tell(ring_sem, px)

    @pl.when(x != 2)
    def _():
        pl.semaphore_wait(ring_sem, 1)

    def meet_z():
        @pl.when(x == 0)
        def _():
            for o in range(1, 8):
                greet(place(0, y, lax.rem(z + o, 8), core))
            pl.semaphore_wait(barrier, 7)
            for px in (1, 2, 3):
                tell(z_sem, px)

        @pl.when(x != 0)
        def _():
            pl.semaphore_wait(z_sem, 1)

        @pl.when(x == 1)
        def _():
            for o in range(1, 8):
                greet(place(1, lax.rem(y + o, 8), z, core))

        @pl.when(x == 3)
        def _():
            greet((d_core, t))

    def meet_rest():
        @pl.when(x == 1)
        def _():
            pl.semaphore_wait(barrier, 7)
            for px in (0, 2, 3):
                tell(y_sem, px)

        @pl.when(x == 3)
        def _():
            pl.semaphore_wait(barrier, 1)
            for px in (0, 1, 2):
                tell(core_sem, px)

        @pl.when(x != 1)
        def _():
            pl.semaphore_wait(y_sem, 1)

        @pl.when(x != 3)
        def _():
            pl.semaphore_wait(core_sem, 1)

    k_out, k_far = [[], []], []

    def own_keys(j):
        columns = pl.ds(pl.multiple_of(x * 256 + j * 128, 128), 128)
        return pltpu.make_async_copy(k_ref.at[0, :, columns], kb.at[j, zh, x], own_sem.at[j, 0])

    def send_keys(j):
        for o in (2, 1, 3):
            tx = lax.rem(x + o, 4)
            columns = pl.ds(pl.multiple_of(tx * 256 + j * 128, 128), 128)
            k_out[j].append(send(
                k_ref.at[0, :, columns], kb.at[j, zh, x], k_ss.at[j, o], k_rs.at[j, o],
                (d, tx * 2 + zh),
            ))
        go(*k_out[j])
        own_keys(j).start()

    def send_half(j):
        arrive(*k_out[j])
        own_keys(j).wait()
        half = kb.at[j, zh]
        k_far.append(send(half, half, k_ss.at[j, 0], k_rs.at[j, 0], (d, x * 2 + 1 - zh)))
        go(k_far[j])

    def head_sends(h):
        out = []
        for o in (2, 1, 3):
            tx = lax.rem(x + o, 4)
            columns = pl.ds(pl.multiple_of(tx * 1280 + h * 128, 128), 128)
            to = (d, tx * 2 + zh)
            out.append(send(q_ref.at[0, :, columns], qb.at[h, x], q_ss.at[h, o - 1], q_rs.at[h, o - 1], to))
            out.append(send(g_ref.at[0, :, columns], gb.at[h, x], g_ss.at[h, o - 1], g_rs.at[h, o - 1], to))
        return out

    def head_own(h):
        columns = pl.ds(pl.multiple_of(x * 1280 + h * 128, 128), 128)
        return [
            pltpu.make_async_copy(q_ref.at[0, :, columns], qb.at[h, x], q_own.at[h]),
            pltpu.make_async_copy(g_ref.at[0, :, columns], gb.at[h, x], g_own.at[h]),
        ]

    def send_head(h):
        for copy in head_sends(h) + head_own(h):
            copy.start()

    send_keys(0)
    send_keys(1)
    pl.loop(0, AHEAD)(send_head)
    meet_z()
    send_half(0)
    send_half(1)

    key_pos = lax.broadcasted_iota(jnp.int32, (128, 128), 0)
    query_pos = lax.broadcasted_iota(jnp.int32, (128, 128), 1)
    for k in range(4):
        for c in range(2 * k + 2):
            seen = jnp.where(mask_ref[0, 2 * k + zh, c] == 1, 0.0, HIDDEN)
            behind = key_pos + c * 128 <= query_pos + (2 * k + zh) * 128
            bias[k, c * 128 : (c + 1) * 128] = jnp.where(behind, seen, HIDDEN)
    vacc[...] = jnp.zeros_like(vacc)

    scale = math.log2(math.e) / math.sqrt(HEAD)

    def attend(j, h):
        for k in range(4):
            n = (2 * k + 2) * 128
            keys = jnp.concatenate([kb[j, c % 2, c // 2] for c in range(2 * k + 2)], axis=0)
            s = lax.dot_general(
                keys, qb[h, k], (((1,), (1,)), ((), ())), preferred_element_type=F32
            )
            s = s * scale + bias[k, 0:n]
            p = jnp.exp2(s - jnp.max(s, axis=0, keepdims=True))
            w = (p * (1.0 / jnp.sum(p, axis=0, keepdims=True))).astype(BF16)
            vacc[j, 0:n] += jnp.dot(w, gb[h, k], preferred_element_type=F32)

    x_in.wait()

    @pl.loop(0, 8)
    def _(yy):
        turned = jnp.transpose(xin[:, pl.ds(pl.multiple_of(yy * 640, 128), 640)])
        for b in range(8):
            xtl[b, pl.ds(pl.multiple_of(yy * 80, 16), 80)] = turned[b * 80 : (b + 1) * 80]

    x_slot = xt.at[:, pl.ds(pl.multiple_of(core * 512 + x * 128, 128), 128)]
    own_x = pltpu.make_async_copy(xtl.at[x * 2 + core], x_slot, own_sem.at[1, 3])
    own_x.start()

    x_out = []
    for o in (4, 2, 6, 5, 3, 7, 1):
        tx, tc = lax.rem(x + o // 2, 4), lax.rem(core + o % 2, 2)
        x_out.append(send(
            xtl.at[tx * 2 + tc], x_slot,
            x_ss.at[o - 1], x_rs.at[o - 1], (d - core + tc, tx * 2 + zh),
        ))

    def send_x():
        for copy in x_out:
            copy.start()

    sent.extend(x_out)

    z_out = [
        send(vsend.at[j], vrecv.at[j], z_ss.at[j], z_rs.at[j], (d, x * 2 + 1 - zh)) for j in range(2)
    ]

    a_out, f_out = [[], []], [[], []]
    for j in range(2):
        mine_v = v2.at[core, 2 * x + j]
        for o in (2, 1, 3):
            a_out[j].append(send(
                mine_v, mine_v, a_ss.at[j, o], a_rs.at[j, o], (d, lax.rem(x + o, 4) * 2 + zh)
            ))
        f_out[j].append(send(mine_v, mine_v, f_ss.at[j, 0], f_rs.at[j, 0], (d_core, t)))

    def share(j):
        z_out[j].wait_recv()
        for k in range(4):
            near = pl.ds(pl.multiple_of((2 * k + zh) * 128, 128), 128)
            rows = pl.ds(k * 128, 128)
            v2[core, 2 * x + j, rows] = (vacc[j, near] + vrecv[j, rows].astype(F32)).astype(BF16)
        for copy in a_out[j] + f_out[j][:1]:
            copy.start()

    for j in range(2):
        arrive(k_far[j])

        @pl.loop(j * GROUP, (j + 1) * GROUP)
        def _(h):
            for copy in head_sends(h):
                copy.wait_recv()
            for copy in head_own(h):
                copy.wait()

            @pl.when(h < 2 * GROUP - AHEAD)
            def _():
                send_head(h + AHEAD)

            if j == 1:
                @pl.when(h == GROUP)
                def _():
                    meet_rest()

                @pl.when(h == SHARE_AT)
                def _():
                    share(0)

                @pl.when(h == X_AT)
                def _():
                    send_x()

            attend(j, h)

        for k in range(4):
            far = pl.ds(pl.multiple_of((2 * k + 1 - zh) * 128, 128), 128)
            vsend[j, k * 128 : (k + 1) * 128] = vacc[j, far].astype(BF16)
        z_out[j].start()

    def forward(j):
        for o, copy in zip((2, 1, 3), a_out[j]):
            copy.wait_recv()
            block = v2.at[core, 2 * lax.rem(x + 4 - o, 4) + j]
            f_out[j].append(send(block, block, f_ss.at[j, o], f_rs.at[j, o], (d_core, t)))
            f_out[j][-1].start()

    def multiply(j):
        for copy in f_out[j]:
            copy.wait_recv()

        @pl.loop(0, 2)
        def _(xx):
            for r in range(4):
                rows = slice(r * 160, (r + 1) * 160)
                total = jnp.zeros((160, 256), F32)
                for cs in range(2):
                    values = jnp.concatenate([v2[cs, 4 * xx + j], v2[cs, 4 * xx + 2 + j]], axis=1)
                    total += jnp.dot(
                        xt[rows, cs * 512 : (cs + 1) * 512], values, preferred_element_type=F32
                    )
                total = total.astype(BF16)
                for cc in range(2):
                    for hh in range(2):
                        block = total[cc * 80 : (cc + 1) * 80, hh * 128 : (hh + 1) * 128]
                        if cc == hh:
                            ca[j, 2 * r + cc, xx] = block
                        else:
                            cb[j, (r // 2) * 4 + 2 * xx + hh, r % 2] = block

    ra_out, rb_out = [[], []], [[], []]

    def first_sum(j):
        for o in (4, 3, 5, 2, 6, 1, 7):
            ty, tz = lax.rem(y + o, 8), lax.rem(z + o, 8)
            ra_out[j].append(send(
                ca.at[j, ty], ra.at[j, y], ra_ss.at[j, o - 1], ra_rs.at[j, o - 1],
                place(x, ty, z, core),
            ))
            rb_out[j].append(send(
                cb.at[j, tz], rb.at[j, z], rb_ss.at[j, o - 1], rb_rs.at[j, o - 1],
                place(x, y, tz, core),
            ))
        go(*rb_out[j])
        go(*ra_out[j])

    fin_out = []

    def second_sum(j, by_z):
        arrive(*(rb_out if by_z else ra_out)[j])
        own_part, parts, me, out, slot = (cb, rb, z, sb, y) if by_z else (ca, ra, y, sa, z)
        for m in range(2):
            total = own_part[j, me, m].astype(F32)
            for o in range(1, 8):
                total += parts[j, lax.rem(me + o, 8), m].astype(F32)
            out[j, m] = total.astype(BF16)
            i = j * 4 + 2 * by_z + m
            to = dest[i]
            copy = send(out.at[j, m], fin.at[slot], fin_ss.at[i], fin_rs.at[slot], place(*to))
            fin_out.append((copy, to))
            here = mine(*to)

            @pl.when(here)
            def _():
                fin[slot] = out[j, m]

            @pl.when(jnp.logical_not(here))
            def _():
                copy.start()

    share(1)
    forward(0)
    for copy in x_out:
        copy.wait_recv()
    own_x.wait()
    multiply(0)
    first_sum(0)
    forward(1)
    for g in range(8):
        vgrad_ref[0, :, g * 128 : (g + 1) * 128] = v2[core, g, pl.ds(pl.multiple_of(x * 128, 128), 128)]
    multiply(1)
    first_sum(1)
    for j in range(2):
        second_sum(j, True)
        second_sum(j, False)

    for s, source in enumerate(sources):
        @pl.when(jnp.logical_not(mine(*source)))
        def _():
            send(sa.at[0, 0], fin.at[s], fin_ss.at[0], fin_rs.at[s], place(*source)).wait_recv()

        parts_ref[s] = fin[s]

    finish()
    for copy in z_out + a_out[0] + a_out[1] + f_out[0] + f_out[1]:
        copy.wait_send()

    @pl.loop(0, 2 * GROUP)
    def _(h):
        for copy in head_sends(h):
            copy.wait_send()

    for copy, to in fin_out:
        @pl.when(jnp.logical_not(mine(*to)))
        def _():
            copy.wait_send()


def add_parts(values_ref, parts_ref, vgrad_ref, wgrad_ref):
    vgrad_ref[...] = values_ref[...]
    total = parts_ref[0].astype(F32)
    for s in range(1, 8):
        total += parts_ref[s].astype(F32)
    wgrad_ref[...] = total * (1.0 / 64.0)


def body(query_states, key_states, out_grad, layer_input, block_mask):
    vmem, dma, regular = pltpu.VMEM, pltpu.SemaphoreType.DMA, pltpu.SemaphoreType.REGULAR
    values, parts = pl.pallas_call(
        kernel,
        out_shape=(
            jax.ShapeDtypeStruct((1, 128, 1024), BF16),
            jax.ShapeDtypeStruct((8, 80, 128), BF16),
        ),
        in_specs=[pl.BlockSpec(memory_space=pltpu.HBM)] * 4 + [pl.BlockSpec(memory_space=pltpu.SMEM)],
        out_specs=(pl.BlockSpec(memory_space=vmem), pl.BlockSpec(memory_space=vmem)),
        scratch_shapes=[
            vmem((10, 4, 128, 128), BF16),
            vmem((10, 4, 128, 128), BF16),
            vmem((2, 2, 4, 128, 128), BF16),
            vmem((128, 5120), BF16),
            vmem((8, 640, 128), BF16),
            vmem((640, 1024), BF16),
            vmem((4, 1024, 128), F32),
            vmem((2, 1024, 128), F32),
            vmem((2, 512, 128), BF16),
            vmem((2, 512, 128), BF16),
            vmem((2, 8, 512, 128), BF16),
            vmem((2, 8, 2, 80, 128), BF16),
            vmem((2, 8, 2, 80, 128), BF16),
            vmem((2, 8, 2, 80, 128), BF16),
            vmem((2, 8, 2, 80, 128), BF16),
            vmem((2, 2, 80, 128), BF16),
            vmem((2, 2, 80, 128), BF16),
            vmem((8, 80, 128), BF16),
            regular, regular, regular, regular,
            dma((2, 4)),
            dma((10,)), dma((10,)),
            dma((2, 4)), dma((2, 4)), dma((10, 3)), dma((10, 3)), dma((10, 3)), dma((10, 3)),
            dma((7,)), dma((7,)), dma((2,)), dma((2,)), dma((2, 4)), dma((2, 4)),
            dma((2, 4)), dma((2, 4)), dma((2, 7)), dma((2, 7)), dma((2, 7)), dma((2, 7)),
            dma((8,)), dma((8,)),
        ],
        compiler_params=pltpu.CompilerParams(
            collective_id=0, has_side_effects=True, vmem_limit_bytes=60 * 2**20
        ),
        name="value_path",
    )(query_states, key_states, out_grad, layer_input, block_mask)
    return pl.pallas_call(
        add_parts,
        out_shape=(
            jax.ShapeDtypeStruct((1, 128, 1024), BF16),
            jax.ShapeDtypeStruct((80, 128), F32),
        ),
        name="add_parts",
    )(values, parts)


def solution(mesh):
    in_specs = (
        P("dp", "ctx", None),
        P("dp", "ctx", None),
        P("dp", "ctx", None),
        P("dp", "ctx", None),
        P("dp", None, None),
    )
    out_specs = (P("dp", "ctx", None), P("dp", "ctx"))
    return jax.shard_map(body, mesh=mesh, in_specs=in_specs, out_specs=out_specs, check_vma=False)
```

```python
import functools
import math

import jax
import jax.numpy as jnp
from jax import lax
from jax.experimental import pallas as pl
from jax.experimental.pallas import tpu as pltpu
from jax.sharding import PartitionSpec as P

HEAD = 128
GROUP = 5
BF16 = jnp.bfloat16
F32 = jnp.float32
MESH = pl.DeviceIdType.MESH
HIDDEN = -1e30
X_AT = 9
SHARE_AT = 8
AHEAD = 5


def kernel(
    q_ref, k_ref, g_ref, x_ref, mask_ref, vgrad_ref, parts_ref,
    qb, gb, kb, xin, xtl, xt, bias, vacc, vsend, vrecv, v2, ca, cb, ra, rb, sa, sb, fin,
    ring_sem, z_sem, y_sem, core_sem, own_sem, q_own, g_own, k_ss, k_rs, q_ss, q_rs, g_ss, g_rs, x_ss, x_rs, z_ss, z_rs, a_ss, a_rs,
    f_ss, f_rs, ra_ss, ra_rs, rb_ss, rb_rs, fin_ss, fin_rs,
):
    d = lax.axis_index("dp")
    t = lax.axis_index("ctx")
    core = lax.rem(d, 2)
    zl = lax.rem(lax.div(d, 2), 4)
    y = lax.div(d, 8)
    x = lax.div(t, 2)
    zh = lax.rem(t, 2)
    z = zh * 4 + zl
    d_core = d + 1 - 2 * core
    y_odd = lax.rem(y, 2)
    zl_odd = lax.rem(zl, 2)

    def place(px, py, pz, pc):
        return ((py * 4 + lax.rem(pz, 4)) * 2 + pc, px * 2 + lax.div(pz, 4))

    def mine(px, py, pz, pc):
        dd, tt = place(px, py, pz, pc)
        return jnp.logical_and(dd == d, tt == t)

    def send(src, dst, ss, rs, to):
        return pltpu.make_async_remote_copy(
            src_ref=src, dst_ref=dst, send_sem=ss, recv_sem=rs, device_id=to, device_id_type=MESH
        )

    x_in = pltpu.make_async_copy(x_ref.at[0], xin, own_sem.at[0, 3])
    x_in.start()

    dest = []
    for j in range(2):
        for m in range(2):
            dest.append((2 * m + y_odd, y, j * 4 + x, core))
        for n in range(2):
            dest.append((zl, 4 * zh + 2 * n + 1 - zl_odd, j * 4 + x, core))
    y_first = lax.rem(x + y, 2) == 0
    half_z = lax.div(y, 4) * 4 + x
    sources = [
        (zl, jnp.where(y_first, y, s), jnp.where(y_first, s, half_z), core) for s in range(8)
    ]

    sent, open_recv = [], []

    def go(*copies):
        for copy in copies:
            copy.start()
            sent.append(copy)
            open_recv.append(copy)

    def arrive(*copies):
        for copy in copies:
            copy.wait_recv()
            open_recv[:] = [other for other in open_recv if other is not copy]

    def finish():
        for copy in open_recv:
            copy.wait_recv()
        for copy in sent:
            copy.wait_send()

    barrier = pltpu.get_barrier_semaphore()

    def greet(to):
        pl.semaphore_signal(barrier, inc=1, device_id=to, device_id_type=MESH)

    def tell(sem, px):
        pl.semaphore_signal(sem, inc=1, device_id=(d, px * 2 + zh), device_id_type=MESH)

    @pl.when(x != 2)
    def _():
        greet((d, 4 + zh))

    @pl.when(x == 2)
    def _():
        pl.semaphore_wait(barrier, 3)
        for px in (0, 1, 3):
            tell(ring_sem, px)

    @pl.when(x != 2)
    def _():
        pl.semaphore_wait(ring_sem, 1)

    def meet_z():
        @pl.when(x == 0)
        def _():
            for o in range(1, 8):
                greet(place(0, y, lax.rem(z + o, 8), core))
            pl.semaphore_wait(barrier, 7)
            for px in (1, 2, 3):
                tell(z_sem, px)

        @pl.when(x != 0)
        def _():
            pl.semaphore_wait(z_sem, 1)

        @pl.when(x == 1)
        def _():
            for o in range(1, 8):
                greet(place(1, lax.rem(y + o, 8), z, core))

        @pl.when(x == 3)
        def _():
            greet((d_core, t))

    def meet_rest():
        @pl.when(x == 1)
        def _():
            pl.semaphore_wait(barrier, 7)
            for px in (0, 2, 3):
                tell(y_sem, px)

        @pl.when(x == 3)
        def _():
            pl.semaphore_wait(barrier, 1)
            for px in (0, 1, 2):
                tell(core_sem, px)

        @pl.when(x != 1)
        def _():
            pl.semaphore_wait(y_sem, 1)

        @pl.when(x != 3)
        def _():
            pl.semaphore_wait(core_sem, 1)

    k_out, k_far = [[], []], []

    def own_keys(j):
        columns = pl.ds(pl.multiple_of(x * 256 + j * 128, 128), 128)
        return pltpu.make_async_copy(k_ref.at[0, :, columns], kb.at[j, zh, x], own_sem.at[j, 0])

    def send_keys(j):
        for o in (2, 1, 3):
            tx = lax.rem(x + o, 4)
            columns = pl.ds(pl.multiple_of(tx * 256 + j * 128, 128), 128)
            k_out[j].append(send(
                k_ref.at[0, :, columns], kb.at[j, zh, x], k_ss.at[j, o], k_rs.at[j, o],
                (d, tx * 2 + zh),
            ))
        go(*k_out[j])
        own_keys(j).start()

    def send_half(j):
        arrive(*k_out[j])
        own_keys(j).wait()
        half = kb.at[j, zh]
        k_far.append(send(half, half, k_ss.at[j, 0], k_rs.at[j, 0], (d, x * 2 + 1 - zh)))
        go(k_far[j])

    def head_sends(h):
        out = []
        for o in (2, 1, 3):
            tx = lax.rem(x + o, 4)
            columns = pl.ds(pl.multiple_of(tx * 1280 + h * 128, 128), 128)
            to = (d, tx * 2 + zh)
            out.append(send(q_ref.at[0, :, columns], qb.at[h, x], q_ss.at[h, o - 1], q_rs.at[h, o - 1], to))
            out.append(send(g_ref.at[0, :, columns], gb.at[h, x], g_ss.at[h, o - 1], g_rs.at[h, o - 1], to))
        return out

    def head_own(h):
        columns = pl.ds(pl.multiple_of(x * 1280 + h * 128, 128), 128)
        return [
            pltpu.make_async_copy(q_ref.at[0, :, columns], qb.at[h, x], q_own.at[h]),
            pltpu.make_async_copy(g_ref.at[0, :, columns], gb.at[h, x], g_own.at[h]),
        ]

    def send_head(h):
        for copy in head_sends(h) + head_own(h):
            copy.start()

    send_keys(0)
    send_keys(1)
    pl.loop(0, AHEAD)(send_head)
    meet_z()
    send_half(0)
    send_half(1)

    key_pos = lax.broadcasted_iota(jnp.int32, (128, 128), 0)
    query_pos = lax.broadcasted_iota(jnp.int32, (128, 128), 1)
    for k in range(4):
        for c in range(2 * k + 2):
            seen = jnp.where(mask_ref[0, 2 * k + zh, c] == 1, 0.0, HIDDEN)
            behind = key_pos + c * 128 <= query_pos + (2 * k + zh) * 128
            bias[k, c * 128 : (c + 1) * 128] = jnp.where(behind, seen, HIDDEN)
    vacc[...] = jnp.zeros_like(vacc)

    scale = math.log2(math.e) / math.sqrt(HEAD)

    def attend(j, h):
        for k in range(4):
            n = (2 * k + 2) * 128
            keys = jnp.concatenate([kb[j, c % 2, c // 2] for c in range(2 * k + 2)], axis=0)
            s = lax.dot_general(
                keys, qb[h, k], (((1,), (1,)), ((), ())), preferred_element_type=F32
            )
            s = s * scale + bias[k, 0:n]
            p = jnp.exp2(s - jnp.max(s, axis=0, keepdims=True))
            w = (p * (1.0 / jnp.sum(p, axis=0, keepdims=True))).astype(BF16)
            vacc[j, 0:n] += jnp.dot(w, gb[h, k], preferred_element_type=F32)

    x_in.wait()

    @pl.loop(0, 8)
    def _(yy):
        turned = jnp.transpose(xin[:, pl.ds(pl.multiple_of(yy * 640, 128), 640)])
        for b in range(8):
            xtl[b, pl.ds(pl.multiple_of(yy * 80, 16), 80)] = turned[b * 80 : (b + 1) * 80]

    x_slot = xt.at[:, pl.ds(pl.multiple_of(core * 512 + x * 128, 128), 128)]
    own_x = pltpu.make_async_copy(xtl.at[x * 2 + core], x_slot, own_sem.at[1, 3])
    own_x.start()

    x_out = []
    for o in (4, 2, 6, 5, 3, 7, 1):
        tx, tc = lax.rem(x + o // 2, 4), lax.rem(core + o % 2, 2)
        x_out.append(send(
            xtl.at[tx * 2 + tc], x_slot,
            x_ss.at[o - 1], x_rs.at[o - 1], (d - core + tc, tx * 2 + zh),
        ))

    def send_x():
        for copy in x_out:
            copy.start()

    sent.extend(x_out)

    z_out = [
        send(vsend.at[j], vrecv.at[j], z_ss.at[j], z_rs.at[j], (d, x * 2 + 1 - zh)) for j in range(2)
    ]

    a_out, f_out = [[], []], [[], []]
    for j in range(2):
        mine_v = v2.at[core, 2 * x + j]
        for part in range(2):
            some = mine_v.at[pl.ds(part * 256, 256)]
            for o in (2, 1, 3):
                a_out[j].append(send(
                    some, some, a_ss.at[j, part, o], a_rs.at[j, part, o],
                    (d, lax.rem(x + o, 4) * 2 + zh),
                ))
        f_out[j].append(send(mine_v, mine_v, f_ss.at[j, 0, 0], f_rs.at[j, 0, 0], (d_core, t)))

    def share(j):
        z_out[j].wait_recv()
        for k in range(4):
            near = pl.ds(pl.multiple_of((2 * k + zh) * 128, 128), 128)
            rows = pl.ds(k * 128, 128)
            v2[core, 2 * x + j, rows] = (vacc[j, near] + vrecv[j, rows].astype(F32)).astype(BF16)
        for copy in a_out[j] + f_out[j][:1]:
            copy.start()

    for j in range(2):
        arrive(k_far[j])

        @pl.loop(j * GROUP, (j + 1) * GROUP)
        def _(h):
            for copy in head_sends(h):
                copy.wait_recv()
            for copy in head_own(h):
                copy.wait()

            @pl.when(h < 2 * GROUP - AHEAD)
            def _():
                send_head(h + AHEAD)

            if j == 1:
                @pl.when(h == GROUP)
                def _():
                    meet_rest()

                @pl.when(h == SHARE_AT)
                def _():
                    share(0)

                @pl.when(h == X_AT)
                def _():
                    send_x()

            attend(j, h)

        for k in range(4):
            far = pl.ds(pl.multiple_of((2 * k + 1 - zh) * 128, 128), 128)
            vsend[j, k * 128 : (k + 1) * 128] = vacc[j, far].astype(BF16)
        z_out[j].start()

    def forward(j):
        for i, copy in enumerate(a_out[j]):
            part, o = i // 3, (2, 1, 3)[i % 3]
            copy.wait_recv()
            block = v2.at[core, 2 * lax.rem(x + 4 - o, 4) + j, pl.ds(part * 256, 256)]
            f_out[j].append(send(
                block, block, f_ss.at[j, part, o], f_rs.at[j, part, o], (d_core, t)
            ))
            f_out[j][-1].start()

    def multiply(j):
        for copy in f_out[j]:
            copy.wait_recv()

        @pl.loop(0, 2)
        def _(xx):
            for r in range(4):
                rows = slice(r * 160, (r + 1) * 160)
                total = jnp.zeros((160, 256), F32)
                for cs in range(2):
                    values = jnp.concatenate([v2[cs, 4 * xx + j], v2[cs, 4 * xx + 2 + j]], axis=1)
                    total += jnp.dot(
                        xt[rows, cs * 512 : (cs + 1) * 512], values, preferred_element_type=F32
                    )
                total = total.astype(BF16)
                for cc in range(2):
                    for hh in range(2):
                        block = total[cc * 80 : (cc + 1) * 80, hh * 128 : (hh + 1) * 128]
                        if cc == hh:
                            ca[j, 2 * r + cc, xx] = block
                        else:
                            cb[j, (r // 2) * 4 + 2 * xx + hh, r % 2] = block

    ra_out, rb_out = [[], []], [[], []]

    def first_sum(j):
        for o in (4, 3, 5, 2, 6, 1, 7):
            ty, tz = lax.rem(y + o, 8), lax.rem(z + o, 8)
            ra_out[j].append(send(
                ca.at[j, ty], ra.at[j, y], ra_ss.at[j, o - 1], ra_rs.at[j, o - 1],
                place(x, ty, z, core),
            ))
            rb_out[j].append(send(
                cb.at[j, tz], rb.at[j, z], rb_ss.at[j, o - 1], rb_rs.at[j, o - 1],
                place(x, y, tz, core),
            ))
        go(*rb_out[j])
        go(*ra_out[j])

    fin_out = []

    def second_sum(j, by_z):
        arrive(*(rb_out if by_z else ra_out)[j])
        own_part, parts, me, out, slot = (cb, rb, z, sb, y) if by_z else (ca, ra, y, sa, z)
        for m in range(2):
            total = own_part[j, me, m].astype(F32)
            for o in range(1, 8):
                total += parts[j, lax.rem(me + o, 8), m].astype(F32)
            out[j, m] = total.astype(BF16)
            i = j * 4 + 2 * by_z + m
            to = dest[i]
            copy = send(out.at[j, m], fin.at[slot], fin_ss.at[i], fin_rs.at[slot], place(*to))
            fin_out.append((copy, to))
            here = mine(*to)

            @pl.when(here)
            def _():
                fin[slot] = out[j, m]

            @pl.when(jnp.logical_not(here))
            def _():
                copy.start()

    share(1)
    forward(0)
    for copy in x_out:
        copy.wait_recv()
    own_x.wait()
    multiply(0)
    first_sum(0)
    forward(1)
    for g in range(8):
        vgrad_ref[0, :, g * 128 : (g + 1) * 128] = v2[core, g, pl.ds(pl.multiple_of(x * 128, 128), 128)]
    multiply(1)
    first_sum(1)
    for j in range(2):
        second_sum(j, True)
        second_sum(j, False)

    for s, source in enumerate(sources):
        @pl.when(jnp.logical_not(mine(*source)))
        def _():
            send(sa.at[0, 0], fin.at[s], fin_ss.at[0], fin_rs.at[s], place(*source)).wait_recv()

        parts_ref[s] = fin[s]

    finish()
    for copy in z_out + a_out[0] + a_out[1] + f_out[0] + f_out[1]:
        copy.wait_send()

    @pl.loop(0, 2 * GROUP)
    def _(h):
        for copy in head_sends(h):
            copy.wait_send()

    for copy, to in fin_out:
        @pl.when(jnp.logical_not(mine(*to)))
        def _():
            copy.wait_send()


def add_parts(values_ref, parts_ref, vgrad_ref, wgrad_ref):
    vgrad_ref[...] = values_ref[...]
    total = parts_ref[0].astype(F32)
    for s in range(1, 8):
        total += parts_ref[s].astype(F32)
    wgrad_ref[...] = total * (1.0 / 64.0)


def body(query_states, key_states, out_grad, layer_input, block_mask):
    vmem, dma, regular = pltpu.VMEM, pltpu.SemaphoreType.DMA, pltpu.SemaphoreType.REGULAR
    values, parts = pl.pallas_call(
        kernel,
        out_shape=(
            jax.ShapeDtypeStruct((1, 128, 1024), BF16),
            jax.ShapeDtypeStruct((8, 80, 128), BF16),
        ),
        in_specs=[pl.BlockSpec(memory_space=pltpu.HBM)] * 4 + [pl.BlockSpec(memory_space=pltpu.SMEM)],
        out_specs=(pl.BlockSpec(memory_space=vmem), pl.BlockSpec(memory_space=vmem)),
        scratch_shapes=[
            vmem((10, 4, 128, 128), BF16),
            vmem((10, 4, 128, 128), BF16),
            vmem((2, 2, 4, 128, 128), BF16),
            vmem((128, 5120), BF16),
            vmem((8, 640, 128), BF16),
            vmem((640, 1024), BF16),
            vmem((4, 1024, 128), F32),
            vmem((2, 1024, 128), F32),
            vmem((2, 512, 128), BF16),
            vmem((2, 512, 128), BF16),
            vmem((2, 8, 512, 128), BF16),
            vmem((2, 8, 2, 80, 128), BF16),
            vmem((2, 8, 2, 80, 128), BF16),
            vmem((2, 8, 2, 80, 128), BF16),
            vmem((2, 8, 2, 80, 128), BF16),
            vmem((2, 2, 80, 128), BF16),
            vmem((2, 2, 80, 128), BF16),
            vmem((8, 80, 128), BF16),
            regular, regular, regular, regular,
            dma((2, 4)),
            dma((10,)), dma((10,)),
            dma((2, 4)), dma((2, 4)), dma((10, 3)), dma((10, 3)), dma((10, 3)), dma((10, 3)),
            dma((7,)), dma((7,)), dma((2,)), dma((2,)), dma((2, 2, 4)), dma((2, 2, 4)),
            dma((2, 2, 4)), dma((2, 2, 4)), dma((2, 7)), dma((2, 7)), dma((2, 7)), dma((2, 7)),
            dma((8,)), dma((8,)),
        ],
        compiler_params=pltpu.CompilerParams(
            collective_id=0, has_side_effects=True, vmem_limit_bytes=60 * 2**20
        ),
        name="value_path",
    )(query_states, key_states, out_grad, layer_input, block_mask)
    return pl.pallas_call(
        add_parts,
        out_shape=(
            jax.ShapeDtypeStruct((1, 128, 1024), BF16),
            jax.ShapeDtypeStruct((80, 128), F32),
        ),
        name="add_parts",
    )(values, parts)


def solution(mesh):
    in_specs = (
        P("dp", "ctx", None),
        P("dp", "ctx", None),
        P("dp", "ctx", None),
        P("dp", "ctx", None),
        P("dp", None, None),
    )
    out_specs = (P("dp", "ctx", None), P("dp", "ctx"))
    return jax.shard_map(body, mesh=mesh, in_specs=in_specs, out_specs=out_specs, check_vma=False)
```
